32 devices in a mesh: parts: 2 (over y), tensor: 16 (over z, x, core).
Axes of the slice: x: 2, y: 2, z: 4, core: 2. Of those that a mesh axis runs over, the one named last changes fastest.
Arguments:
- hidden_in: bfloat16 [2048, 5120], P('parts', 'tensor'), parts along dimension 0, may hold values from -6 to 6
- out_grad: bfloat16 [2048, 5120], P('parts', 'tensor'), parts along dimension 0, may hold values from -6 to 6
- w_gate: bfloat16 [5120, 13824], P(None, 'tensor'), may hold values from -0.078125 to 0.078125
- w_up: bfloat16 [5120, 13824], P(None, 'tensor'), may hold values from -0.078125 to 0.078125
- w_down: bfloat16 [13824, 5120], P('tensor'), may hold values from -0.0546875 to 0.0546875
- proj_in: bfloat16 [5120, 64], replicated, may hold values from -0.078125 to 0.078125
- proj_ff: bfloat16 [13824, 64], P('tensor'), may hold values from -0.0546875 to 0.0546875
- proj_out: bfloat16 [5120, 64], replicated, may hold values from -0.078125 to 0.078125
- lengths: int32 [16], P('parts'), parts along dimension 0, may hold values from 1 to 256, 1024 in all
Outputs:
- example_grads: float32 [16, 12288], P('parts'), parts along dimension 0
The draws below stay inside these ranges and needn't reach their ends.
There are 2 independent parts, one for each index of `parts`. The reference program is written for one: setup_inputs(seed, part) draws one part's arguments, and reference() takes and returns one part's arrays. A program takes and returns all parts, laid end to end along the dimension named above; an argument that names none is the same for every part. Nothing has to cross between parts.
Inputs may be any that keep to these rules, and one draw needn't show every extreme that they name: The lengths sum to 1024, and the longest sequence has exactly 256 tokens.
All inputs are finite; a program needn't handle non-finite values.
Results may differ from the reference program's by a relative error of at most 0.0023.
Values may be sent and summed in bfloat16 or wider, within the bound.
A program may use at most 128 MiB of HBM per device.

```python
import math
import jax
import jax.numpy as jnp
import numpy as np
from jax import lax

D = 5120
FF = 13824
R = 64
SEGS = 8
TOKENS = 1024
MOST = 256


def block_levels(stream_key, dims, split, smallest, top_value):
    factor_of = 1.0
    for dim, parts in split:
        steps = jax.random.uniform(jax.random.fold_in(jax.random.fold_in(stream_key, 6), dim), (parts,), jnp.float32, smallest / len(split), top_value / len(split))
        factor_of = factor_of * jnp.repeat(jnp.exp(steps), dims[dim] // parts).reshape((-1,) + (1,) * (len(dims) - 1 - dim))
    return factor_of


def profile(amount, total, bound, skew):
    weights = [(1 << 20) // math.isqrt(standing ** skew) + 1 for standing in range(2, amount + 1)]
    rest, holding = total - bound - (amount - 1), [1] * (amount - 1)
    while rest > 0:
        free = [i for i in range(amount - 1) if holding[i] < bound]
        whole, left = sum([weights[i] for i in free]), rest
        for i in free:
            extra = min(bound - holding[i], max(1, left * weights[i] // whole), rest)
            holding[i] = holding[i] + extra
            rest = rest - extra
    return np.array([bound] + holding)


def ragged_sizes(own_key, amount, total, reach, skew):
    if amount == 2:
        one = jax.random.randint(own_key, (), max(1, total - reach), min(reach, total - 1) + 1)
        return jnp.stack([one, total - one])
    sizes = jnp.asarray(profile(amount, total, reach, skew), jnp.int32)
    pairs = (amount - 1) // 2
    giver, sink = sizes[1:1 + 2 * pairs:2], sizes[2:2 + 2 * pairs:2]
    slack = jnp.minimum(giver - 1, reach - sink)
    passed = jax.random.randint(jax.random.fold_in(own_key, 1), (pairs,), 0, 1 << 20) % (slack + 1)
    sizes = sizes.at[1:1 + 2 * pairs:2].set(giver - passed).at[2:2 + 2 * pairs:2].set(sink + passed)
    return sizes[jax.random.permutation(jax.random.fold_in(own_key, 2), amount)]


def normal_values(rng, shape, scale, most, split=(), kind=jnp.bfloat16):
    level = block_levels(rng, shape, split, -0.22, 0.18) if split else 1.0
    result = jax.random.normal(rng, shape, jnp.float32) * scale * level
    return jnp.minimum(jnp.maximum(result, -most), most).astype(kind)


def setup_inputs(seed: int = 0, part: int = 0) -> dict:
    seeds = jax.random.split(jax.random.key(seed), 10)
    part_keys = jax.random.split(jax.random.fold_in(seeds[9], part), 10)
    hidden_in = normal_values(part_keys[0], (TOKENS, D), 1.0, 6.0, ((1, 16),))
    out_grad = normal_values(part_keys[1], (TOKENS, D), 1.0, 6.0, ((1, 16),))
    w_gate = normal_values(seeds[2], (D, FF), D ** -0.5, 0.078125, ((1, 16),))
    w_up = normal_values(seeds[3], (D, FF), D ** -0.5, 0.078125, ((1, 16),))
    w_down = normal_values(seeds[4], (FF, D), FF ** -0.5, 0.0546875, ((0, 16),))
    proj_in = normal_values(seeds[5], (D, R), D ** -0.5, 0.078125)
    proj_ff = normal_values(seeds[6], (FF, R), FF ** -0.5, 0.0546875, ((0, 16),))
    proj_out = normal_values(seeds[7], (D, R), D ** -0.5, 0.078125)
    lengths = ragged_sizes(part_keys[8], SEGS, TOKENS, MOST, 2).astype(jnp.int32)
    return {"hidden_in": hidden_in, "out_grad": out_grad, "w_gate": w_gate, "w_up": w_up, "w_down": w_down, "proj_in": proj_in, "proj_ff": proj_ff, "proj_out": proj_out, "lengths": lengths}


def outer_sums(table, grads, inputs):
    rows = table.shape[0]
    segs = table.shape[1]
    width = grads.shape[1]
    weighted = (table[:, :, None] * grads[:, None, :]).reshape(rows, segs * width)
    summed = jnp.dot(weighted.T, inputs, precision=lax.Precision.HIGHEST, preferred_element_type=jnp.float32)
    return summed.reshape(segs, width * inputs.shape[1])


def reference(hidden_in, out_grad, w_gate, w_up, w_down, proj_in, proj_ff, proj_out, lengths):
    gate_pre = jnp.dot(hidden_in, w_gate, preferred_element_type=jnp.float32)
    up_pre = jnp.dot(hidden_in, w_up, preferred_element_type=jnp.float32)
    sigma = jax.nn.sigmoid(gate_pre)
    active = gate_pre * sigma
    hidden = (active * up_pre).astype(jnp.bfloat16)
    hidden_grad = jnp.dot(out_grad, w_down.T, preferred_element_type=jnp.float32)
    gate_grad = hidden_grad * up_pre * sigma * (1.0 + gate_pre * (1.0 - sigma))
    up_grad = hidden_grad * active
    ff_float = proj_ff.astype(jnp.float32)
    hid_proj = jnp.dot(hidden, proj_ff, preferred_element_type=jnp.float32)
    gate_proj = jnp.dot(gate_grad, ff_float, precision=lax.Precision.HIGHEST, preferred_element_type=jnp.float32)
    up_proj = jnp.dot(up_grad, ff_float, precision=lax.Precision.HIGHEST, preferred_element_type=jnp.float32)
    in_proj = jnp.dot(hidden_in, proj_in, preferred_element_type=jnp.float32)
    grad_proj = jnp.dot(out_grad, proj_out, preferred_element_type=jnp.float32)
    ends = jnp.cumsum(lengths).astype(jnp.int32)
    position = jnp.arange(TOKENS, dtype=jnp.int32)
    segment = jnp.sum((position[:, None] >= ends[None, :]).astype(jnp.int32), axis=1)
    table = (segment[:, None] == jnp.arange(SEGS, dtype=jnp.int32)[None, :]).astype(jnp.float32)
    return jnp.concatenate([outer_sums(table, gate_proj, in_proj), outer_sums(table, up_proj, in_proj), outer_sums(table, grad_proj, hid_proj)], axis=1)
```

```python
import functools

import jax
import jax.numpy as jnp
from jax import lax
from jax.experimental import pallas as pl
from jax.experimental.pallas import tpu as pltpu
from jax.sharding import PartitionSpec as P

CHUNKS = 4
MESH = pl.DeviceIdType.MESH


def ring_chip(pos, chips):
    column = chips // 2
    side = pos // column
    level = pos * (1 - side) + (chips - 1 - pos) * side
    return 2 * level + side


def split_high(value):
    high = value.astype(jnp.bfloat16)
    return high, (value - high.astype(jnp.float32)).astype(jnp.bfloat16)


def fused_kernel(
    chips, segs,
    x_ref, g_ref, wg_hbm, wu_hbm, wd_hbm, pin_ref, pout_ref, pff_ref, table_ref,
    out_ref,
    xbuf, gbuf, xpair, gpair, acc_g, acc_u, acc_b, acc_p, wg, wu, wd,
    hid_s, gg_hi, gg_lo, ug_hi, ug_lo, sums, sib_half, half, pieces, result,
    xp_send, xp_recv, gp_send, gp_recv, x_send, x_recv, g_send, g_recv,
    xs_send, xs_recv, gs_send, gs_recv, w_sem,
    sib_sem, rs_send, rs_recv, ag_send, ag_recv, fw_send, fw_recv,
):
    me = lax.axis_index("tensor")
    core = lax.rem(me, 2)
    chip = me // 2
    side = lax.rem(chip, 2)
    level = chip // 2
    pos = level * (1 - side) + (chips - 1 - level) * side
    right = 2 * ring_chip(lax.rem(pos + 1, chips), chips) + core
    left = 2 * ring_chip(lax.rem(pos + chips - 1, chips), chips) + core
    sib = me + 1 - 2 * core
    last = chips - 1
    total = x_ref.shape[0]
    width = x_ref.shape[1]
    block = 2 * width
    rows = total // CHUNKS
    own = rows // 2
    whole = sums.shape[0]
    part = whole // 2
    piece = part // chips

    barrier = pltpu.get_barrier_semaphore()
    pl.semaphore_signal(barrier, inc=1, device_id={"tensor": sib}, device_id_type=MESH)
    for d in range(1, chips):
        peer = 2 * lax.rem(chip + d, chips) + core
        pl.semaphore_signal(barrier, inc=1, device_id={"tensor": peer}, device_id_type=MESH)

    def weight_copies(step, slot):
        from_x = ring_chip(lax.rem(pos - step + chips, chips), chips)
        from_g = ring_chip(lax.rem(pos + step, chips), chips)
        x_rows = pl.ds(pl.multiple_of(from_x * block, block), block)
        g_cols = pl.ds(pl.multiple_of(from_g * block, block), block)
        return (
            pltpu.make_async_copy(wg_hbm.at[x_rows, :], wg.at[slot], w_sem.at[slot, 0]),
            pltpu.make_async_copy(wu_hbm.at[x_rows, :], wu.at[slot], w_sem.at[slot, 1]),
            pltpu.make_async_copy(wd_hbm.at[:, g_cols], wd.at[slot], w_sem.at[slot, 2]),
        )

    def remote(src, dst, send, recv, device):
        return pltpu.make_async_remote_copy(
            src_ref=src, dst_ref=dst, send_sem=send, recv_sem=recv,
            device_id={"tensor": device}, device_id_type=MESH,
        )

    def chunk_rows(j):
        return pl.ds(pl.multiple_of(j * rows, rows), rows)

    def own_rows(j):
        return pl.ds(pl.multiple_of(j * rows + core * own, own), own)

    def pair_copies(j):
        r = chunk_rows(j)
        return (
            remote(x_ref.at[r, :], xpair.at[r, :], xp_send.at[j], xp_recv.at[j], sib),
            remote(g_ref.at[r, :], gpair.at[r, :], gp_send.at[j], gp_recv.at[j], sib),
        )

    def ring_copies(s, j):
        r = own_rows(j)
        return (
            remote(xbuf.at[s, r, :], xbuf.at[s + 1, r, :], x_send.at[s, j], x_recv.at[s, j], right),
            remote(gbuf.at[s, r, :], gbuf.at[s + 1, r, :], g_send.at[s, j], g_recv.at[s, j], left),
        )

    def sib_copies(s, j):
        r = own_rows(j)
        return (
            remote(xbuf.at[s, r, :], xbuf.at[s, r, :], xs_send.at[s, j], xs_recv.at[s, j], sib),
            remote(gbuf.at[s, r, :], gbuf.at[s, r, :], gs_send.at[s, j], gs_recv.at[s, j], sib),
        )

    for slot in range(2):
        for copy in weight_copies(slot, slot):
            copy.start()
    sums[...] = jnp.zeros_like(sums)
    pl.semaphore_wait(barrier, chips)

    for j in range(CHUNKS):
        for copy in pair_copies(j):
            copy.start()

    for j in range(CHUNKS):
        r = slice(j * rows, (j + 1) * rows)
        for copy in pair_copies(j):
            copy.wait_recv()
        for ref, pair, buf in ((x_ref, xpair, xbuf), (g_ref, gpair, gbuf)):
            mine, other = ref[r, :], pair[r, :]
            first = jnp.where(core == 0, mine, other)
            second = jnp.where(core == 0, other, mine)
            buf[0, r, :] = jnp.concatenate([first, second], axis=1)
        for copy in ring_copies(0, j):
            copy.start()

    def multiply(s, slot, j, start):
        r = chunk_rows(j)
        x = xbuf[s, r, :]
        g = gbuf[s, r, :]
        from_x = ring_chip(lax.rem(pos - s + chips, chips), chips)
        from_g = ring_chip(lax.rem(pos + s, chips), chips)
        x_rows = pl.ds(pl.multiple_of(from_x * block, block), block)
        g_rows = pl.ds(pl.multiple_of(from_g * block, block), block)

        def put(acc, value):
            if start:
                acc[r, :] = value
            else:
                acc[r, :] += value

        put(acc_g, jnp.dot(x, wg[slot], preferred_element_type=jnp.float32))
        put(acc_u, jnp.dot(x, wu[slot], preferred_element_type=jnp.float32))
        put(acc_b, lax.dot_general(
            g, wd[slot], (((1,), (1,)), ((), ())), preferred_element_type=jnp.float32))
        put(acc_p, jnp.dot(x, pin_ref[x_rows, :], preferred_element_type=jnp.float32)
            + jnp.dot(g, pout_ref[g_rows, :], preferred_element_type=jnp.float32))

    for copy in weight_copies(0, 0):
        copy.wait()

    @pl.loop(0, CHUNKS)
    def _(j):
        multiply(0, 0, j, True)

    for copy in weight_copies(2, 0):
        copy.start()

    def finish(j):
        sub = min(32, rows)

        @pl.loop(0, rows // sub)
        def _(i):
            r = pl.ds(pl.multiple_of(j * rows + i * sub, sub), sub)
            o = pl.ds(pl.multiple_of(i * sub, sub), sub)
            gate, up, back = acc_g[r, :], acc_u[r, :], acc_b[r, :]
            sigma = jax.nn.sigmoid(gate)
            active = gate * sigma
            hid_s[o, :] = (active * up).astype(jnp.bfloat16)
            gg_hi[o, :], gg_lo[o, :] = split_high(back * up * sigma * (1.0 + gate * (1.0 - sigma)))
            ug_hi[o, :], ug_lo[o, :] = split_high(back * active)

        def dot(a, b):
            return jnp.dot(a, b, preferred_element_type=jnp.float32)

        both = (dot(gg_hi[...], pff_ref[0]) + dot(gg_lo[...], pff_ref[0])
                + dot(ug_hi[...], pff_ref[1]) + dot(ug_lo[...], pff_ref[1]))
        hidden = dot(hid_s[...], pff_ref[2])
        r = chunk_rows(j)
        turned = acc_p[r, :].T
        t_hi, t_lo = split_high(turned)
        rank = t_hi.shape[0] // 2
        table = table_ref[r, :]
        lane = lax.broadcasted_iota(jnp.int32, both.shape, 1)
        b_hi, b_lo = (v.astype(jnp.float32) for v in split_high(both))
        h_hi, h_lo = (v.astype(jnp.float32) for v in split_high(hidden))
        wide = 2 * rank
        for k in range(segs + segs // 2):
            if k < segs:
                mask = jnp.broadcast_to(table[:, k:k + 1], both.shape)
                hi, lo, a = b_hi, b_lo, slice(0, rank)
            else:
                s = 2 * (k - segs)
                mask = jnp.where(lane < rank, table[:, s:s + 1], table[:, s + 1:s + 2])
                hi, lo, a = h_hi, h_lo, slice(rank, wide)
            hi = (hi * mask).astype(jnp.bfloat16)
            lo = (lo * mask).astype(jnp.bfloat16)
            sums[k * rank:(k + 1) * rank, :] += (
                dot(t_hi[a], hi) + (dot(t_lo[a], hi) + dot(t_hi[a], lo)))

    @pl.loop(1, chips)
    def _(s):
        slot = lax.rem(s, 2)
        for copy in weight_copies(s, slot):
            copy.wait()

        @pl.loop(0, CHUNKS)
        def _(j):
            for copy in ring_copies(s - 1, j):
                copy.wait_recv()

            @pl.when(s < last)
            def _():
                for copy in ring_copies(s, j):
                    copy.start()

            for copy in sib_copies(s, j):
                copy.start()
            for copy in sib_copies(s, j):
                copy.wait_recv()
            multiply(s, slot, j, False)

            @pl.when(s == last)
            def _():
                finish(j)

        @pl.when(s + 2 < chips)
        def _():
            for copy in weight_copies(s + 2, slot):
                copy.start()

    mine = pl.ds(pl.multiple_of(core * part, part), part)
    others = pl.ds(pl.multiple_of((1 - core) * part, part), part)
    swap = remote(sums.at[others, :], sib_half, sib_sem.at[0], sib_sem.at[1], sib)
    swap.start()

    @pl.loop(0, last)
    def _(s):
        @pl.loop(0, CHUNKS)
        def _(j):
            for copy in ring_copies(s, j):
                copy.wait_send()
            for copy in sib_copies(s + 1, j):
                copy.wait_send()

    for j in range(CHUNKS):
        for copy in pair_copies(j):
            copy.wait_send()

    swap.wait_recv()
    half[...] = sums[mine, :] + sib_half[...]

    def piece_rows(c):
        return pl.ds(pl.multiple_of(c * piece, piece), piece)

    def scatter(d):
        to = lax.rem(chip + d, chips)
        return remote(
            half.at[piece_rows(to), :], pieces.at[d], rs_send.at[d], rs_recv.at[d], 2 * to + core)

    for d in range(1, chips):
        scatter(d).start()
    value = half[piece_rows(chip), :]
    for d in range(1, chips):
        scatter(d).wait_recv()
        value = value + pieces[d]

    def result_rows(c, which):
        return pl.ds(pl.multiple_of(which * part + c * piece, piece), piece)

    result[result_rows(chip, core), :] = value

    def spread(d):
        r = result_rows(chip, core)
        to = 2 * lax.rem(chip + d, chips) + core
        return remote(result.at[r, :], result.at[r, :], ag_send.at[d], ag_recv.at[d], to)

    def spread_in(d):
        r = result_rows(lax.rem(chip - d + chips, chips), core)
        to = 2 * lax.rem(chip + d, chips) + core
        return remote(result.at[r, :], result.at[r, :], ag_send.at[d], ag_recv.at[d], to)

    def forward(d, which):
        r = result_rows(lax.rem(chip - d + chips, chips), which)
        return remote(result.at[r, :], result.at[r, :], fw_send.at[d], fw_recv.at[d], sib)

    for d in range(1, chips):
        spread(d).start()
    forward(0, core).start()
    for d in range(1, chips):
        spread_in(d).wait_recv()
        forward(d, core).start()
    for d in range(chips):
        forward(d, 1 - core).wait_recv()
    out_ref[...] = result[...]
    swap.wait_send()
    for d in range(1, chips):
        scatter(d).wait_send()
        spread(d).wait_send()
    for d in range(chips):
        forward(d, core).wait_send()


def fused_sums(chips, hidden_in, out_grad, w_gate, w_up, w_down, pin, pout, pff, table):
    total, width = hidden_in.shape
    units = w_gate.shape[1]
    segs = table.shape[1]
    rank = pin.shape[1] // 2
    block = 2 * width
    rows = total // CHUNKS
    out_rows = rank * (segs + segs // 2)
    bf16, f32 = jnp.bfloat16, jnp.float32
    vmem = pl.BlockSpec(memory_space=pltpu.VMEM)
    hbm = pl.BlockSpec(memory_space=pl.ANY)
    dma = pltpu.SemaphoreType.DMA
    return pl.pallas_call(
        functools.partial(fused_kernel, chips, segs),
        out_shape=jax.ShapeDtypeStruct((out_rows, 2 * rank), f32),
        in_specs=[vmem, vmem, hbm, hbm, hbm, vmem, vmem, vmem, vmem],
        out_specs=vmem,
        scratch_shapes=[
            pltpu.VMEM((chips, total, block), bf16),
            pltpu.VMEM((chips, total, block), bf16),
            pltpu.VMEM((total, width), bf16),
            pltpu.VMEM((total, width), bf16),
            pltpu.VMEM((total, units), f32),
            pltpu.VMEM((total, units), f32),
            pltpu.VMEM((total, units), f32),
            pltpu.VMEM((total, 2 * rank), f32),
            pltpu.VMEM((2, block, units), bf16),
            pltpu.VMEM((2, block, units), bf16),
            pltpu.VMEM((2, units, block), bf16),
        ]
        + [pltpu.VMEM((rows, units), bf16)] * 5
        + [
            pltpu.VMEM((out_rows, 2 * rank), f32),
            pltpu.VMEM((out_rows // 2, 2 * rank), f32),
            pltpu.VMEM((out_rows // 2, 2 * rank), f32),
            pltpu.VMEM((chips, out_rows // 2 // chips, 2 * rank), f32),
            pltpu.VMEM((out_rows, 2 * rank), f32),
        ]
        + [dma((CHUNKS,))] * 4
        + [dma((chips, CHUNKS))] * 8
        + [dma((2, 3)), dma((2,))]
        + [dma((chips,))] * 6,
        compiler_params=pltpu.CompilerParams(
            collective_id=0, has_side_effects=True, vmem_limit_bytes=60 * 1024 * 1024
        ),
    )(hidden_in, out_grad, w_gate, w_up, w_down, pin, pout, pff, table)


def fused_body(hidden_in, out_grad, w_gate, w_up, w_down, proj_in, proj_ff, proj_out, lengths):
    chips = lax.axis_size("tensor") // 2
    rank = proj_in.shape[1]
    segs = lengths.shape[0]
    table = segment_table(lengths, 0, hidden_in.shape[0])
    pin = jnp.pad(proj_in, ((0, 0), (0, rank)))
    pout = jnp.pad(proj_out, ((0, 0), (rank, 0)))
    pff = jnp.stack([
        jnp.pad(proj_ff, ((0, 0), (0, rank))),
        jnp.pad(proj_ff, ((0, 0), (rank, 0))),
        jnp.concatenate([proj_ff, proj_ff], axis=1),
    ])
    sums = fused_sums(chips, hidden_in, out_grad, w_gate, w_up, w_down, pin, pout, pff, table)
    first = sums[:segs * rank].reshape(segs, rank, 2, rank)
    second = sums[segs * rank:].reshape(segs // 2, rank, 2, rank)
    first = first.transpose(0, 2, 3, 1).reshape(segs, 2 * rank * rank)
    second = second.transpose(0, 2, 1, 3).reshape(segs, rank * rank)
    return jnp.concatenate([first, second], axis=1)


def outer_sums(table, grads, inputs):
    rows = table.shape[0]
    segs = table.shape[1]
    width = grads.shape[1]
    weighted = (table[:, :, None] * grads[:, None, :]).reshape(rows, segs * width)
    summed = jnp.dot(
        weighted.T, inputs, precision=lax.Precision.HIGHEST, preferred_element_type=jnp.float32
    )
    return summed.reshape(segs, width * inputs.shape[1])


def segment_table(lengths, start, rows):
    ends = jnp.cumsum(lengths)
    position = start + jnp.arange(rows, dtype=jnp.int32)
    segment = jnp.sum((position[:, None] >= ends[None, :]).astype(jnp.int32), axis=1)
    return (segment[:, None] == jnp.arange(lengths.shape[0], dtype=jnp.int32)[None, :]).astype(
        jnp.float32
    )


def example_sums(table, projected, in_proj, grad_proj, rank):
    hid_proj = projected[:, :rank]
    gate_proj = projected[:, rank : 2 * rank]
    up_proj = projected[:, 2 * rank : 3 * rank]
    return jnp.concatenate(
        [
            outer_sums(table, gate_proj, in_proj),
            outer_sums(table, up_proj, in_proj),
            outer_sums(table, grad_proj, hid_proj),
        ],
        axis=1,
    )


def body(hidden_in, out_grad, w_gate, w_up, w_down, proj_in, proj_ff, proj_out, lengths):
    total_rows = hidden_in.shape[0]
    units = w_gate.shape[1]
    rank = proj_in.shape[1]
    tok_share = total_rows // lax.axis_size("tensor")
    piece = lax.all_gather(hidden_in, "tensor", axis=1, tiled=True)
    pair = jnp.concatenate(
        [
            jnp.dot(piece, w_gate, preferred_element_type=jnp.float32),
            jnp.dot(piece, w_up, preferred_element_type=jnp.float32),
        ],
        axis=1,
    )
    in_proj = jnp.dot(piece, proj_in, preferred_element_type=jnp.float32)
    piece = lax.all_gather(out_grad, "tensor", axis=1, tiled=True)
    back = lax.dot_general(
        piece, w_down, (((1,), (1,)), ((), ())), preferred_element_type=jnp.float32
    )
    grad_proj = jnp.dot(piece, proj_out, preferred_element_type=jnp.float32)
    gate_pre = pair[:, :units]
    up_pre = pair[:, units:]
    sigma = jax.nn.sigmoid(gate_pre)
    active = gate_pre * sigma
    hidden = (active * up_pre).astype(jnp.bfloat16)
    gate_grad = back * up_pre * sigma * (1.0 + gate_pre * (1.0 - sigma))
    up_grad = back * active
    ff_float = proj_ff.astype(jnp.float32)
    shares = lax.psum_scatter(
        jnp.concatenate(
            [
                jnp.dot(hidden, proj_ff, preferred_element_type=jnp.float32),
                jnp.dot(
                    gate_grad,
                    ff_float,
                    precision=lax.Precision.HIGHEST,
                    preferred_element_type=jnp.float32,
                ),
                jnp.dot(
                    up_grad,
                    ff_float,
                    precision=lax.Precision.HIGHEST,
                    preferred_element_type=jnp.float32,
                ),
            ],
            axis=1,
        ),
        "tensor",
        scatter_dimension=0,
        tiled=True,
    )
    first_row = lax.axis_index("tensor") * tok_share
    table = segment_table(lengths, first_row, tok_share)
    in_part = lax.dynamic_slice_in_dim(in_proj, first_row, tok_share, 0)
    grad_part = lax.dynamic_slice_in_dim(grad_proj, first_row, tok_share, 0)
    partial_sums = example_sums(table, shares, in_part, grad_part, rank)
    result = lax.psum(partial_sums, "tensor")
    return result


def solution(mesh):
    placed = (
        P("parts", "tensor"),
        P("parts", "tensor"),
        P(None, "tensor"),
        P(None, "tensor"),
        P("tensor", None),
        P(),
        P("tensor", None),
        P(),
        P("parts"),
    )

    def either(*args):
        devices = lax.axis_size("tensor")
        fits = (
            devices == 16
            and 2 * args[0].shape[1] % 128 == 0
            and args[0].shape[0] % (32 * CHUNKS) == 0
            and args[2].shape[1] % 16 == 0
            and args[5].shape[1] == 64
            and args[8].shape[0] % 2 == 0
        )
        return (fused_body if fits else body)(*args)

    return jax.shard_map(
        either, mesh=mesh, in_specs=placed, out_specs=P("parts", None), check_vma=False
    )
```

```python
import functools

import jax
import jax.numpy as jnp
from jax import lax
from jax.experimental import pallas as pl
from jax.experimental.pallas import tpu as pltpu
from jax.sharding import PartitionSpec as P

CHUNKS = 4
MESH = pl.DeviceIdType.MESH


def ring_chip(pos, chips):
    column = chips // 2
    side = pos // column
    level = pos * (1 - side) + (chips - 1 - pos) * side
    return 2 * level + side


def split_high(value):
    high = value.astype(jnp.bfloat16)
    return high, (value - high.astype(jnp.float32)).astype(jnp.bfloat16)


def fused_kernel(
    chips, segs,
    x_ref, g_ref, wg_hbm, wu_hbm, wd_hbm, pin_ref, pout_ref, pff_ref, table_ref,
    out_ref,
    xbuf, gbuf, acc_g, acc_u, acc_b, acc_p, wg, wu, wd,
    hid_s, gg_hi, gg_lo, ug_hi, ug_lo, sums, packed, sib_half, half, pieces, result,
    xp_send, xp_recv, gp_send, gp_recv, x_send, x_recv, g_send, g_recv,
    xs_send, xs_recv, gs_send, gs_recv, w_sem,
    sib_sem, rs_send, rs_recv, ag_send, ag_recv, fw_send, fw_recv,
):
    me = lax.axis_index("tensor")
    core = lax.rem(me, 2)
    chip = me // 2
    side = lax.rem(chip, 2)
    level = chip // 2
    pos = level * (1 - side) + (chips - 1 - level) * side
    right = 2 * ring_chip(lax.rem(pos + 1, chips), chips) + core
    left = 2 * ring_chip(lax.rem(pos + chips - 1, chips), chips) + core
    sib = me + 1 - 2 * core
    last = chips - 1
    width, total = x_ref.shape
    block = 2 * width
    rows = total // CHUNKS
    own = rows // 2
    part = packed.shape[0] // 2
    piece = part // chips

    barrier = pltpu.get_barrier_semaphore()
    pl.semaphore_signal(barrier, inc=1, device_id={"tensor": sib}, device_id_type=MESH)
    for d in range(1, chips):
        peer = 2 * lax.rem(chip + d, chips) + core
        pl.semaphore_signal(barrier, inc=1, device_id={"tensor": peer}, device_id_type=MESH)

    def weight_copies(step, slot):
        from_x = ring_chip(lax.rem(pos - step + chips, chips), chips)
        from_g = ring_chip(lax.rem(pos + step, chips), chips)
        x_cols = pl.ds(pl.multiple_of(from_x * block, block), block)
        g_cols = pl.ds(pl.multiple_of(from_g * block, block), block)
        return (
            pltpu.make_async_copy(wg_hbm.at[:, x_cols], wg.at[slot], w_sem.at[slot, 0]),
            pltpu.make_async_copy(wu_hbm.at[:, x_cols], wu.at[slot], w_sem.at[slot, 1]),
            pltpu.make_async_copy(wd_hbm.at[:, g_cols], wd.at[slot], w_sem.at[slot, 2]),
        )

    def remote(src, dst, send, recv, device):
        return pltpu.make_async_remote_copy(
            src_ref=src, dst_ref=dst, send_sem=send, recv_sem=recv,
            device_id={"tensor": device}, device_id_type=MESH,
        )

    def chunk(j):
        return pl.ds(pl.multiple_of(j * rows, rows), rows)

    def ring_part(j, which):
        return pl.ds(pl.multiple_of(j * rows + which * own, own), own)

    features = pl.ds(pl.multiple_of(core * width, width), width)

    def pair_copies(j, k):
        c = ring_part(j, (1 - core) * (1 - k) + core * k)
        return (
            remote(x_ref.at[:, c], xbuf.at[0, features, c], xp_send.at[k, j], xp_recv.at[k, j], sib),
            remote(g_ref.at[:, c], gbuf.at[0, features, c], gp_send.at[k, j], gp_recv.at[k, j], sib),
        )

    def ring_copies(s, j):
        c = ring_part(j, core)
        return (
            remote(xbuf.at[s, :, c], xbuf.at[s + 1, :, c], x_send.at[s, j], x_recv.at[s, j], right),
            remote(gbuf.at[s, :, c], gbuf.at[s + 1, :, c], g_send.at[s, j], g_recv.at[s, j], left),
        )

    def sib_copies(s, j):
        c = ring_part(j, core)
        return (
            remote(xbuf.at[s, :, c], xbuf.at[s, :, c], xs_send.at[s, j], xs_recv.at[s, j], sib),
            remote(gbuf.at[s, :, c], gbuf.at[s, :, c], gs_send.at[s, j], gs_recv.at[s, j], sib),
        )

    pl.semaphore_wait(barrier, chips)
    for k in range(2):
        for j in range(CHUNKS):
            for copy in pair_copies(j, k):
                copy.start()
    for slot in range(2):
        for copy in weight_copies(slot, slot):
            copy.start()
    xbuf[0, features, :] = x_ref[...]
    gbuf[0, features, :] = g_ref[...]
    for j in range(CHUNKS):
        for copy in pair_copies(j, 0):
            copy.wait_recv()
        for copy in ring_copies(0, j):
            copy.start()
    sums[...] = jnp.zeros_like(sums)
    for j in range(CHUNKS):
        for copy in pair_copies(j, 1):
            copy.wait_recv()

    def dot(a, b):
        return jnp.dot(a, b, preferred_element_type=jnp.float32)

    def dot_lanes(a, b):
        return lax.dot_general(
            a, b, (((1,), (1,)), ((), ())), preferred_element_type=jnp.float32)

    def multiply(s, slot, j, start):
        c = chunk(j)
        x = xbuf[s, :, c]
        g = gbuf[s, :, c]
        from_x = ring_chip(lax.rem(pos - s + chips, chips), chips)
        from_g = ring_chip(lax.rem(pos + s, chips), chips)
        x_cols = pl.ds(pl.multiple_of(from_x * block, block), block)
        g_cols = pl.ds(pl.multiple_of(from_g * block, block), block)
        rank = pin_ref.shape[0]

        def put(acc, r, value):
            if start:
                acc[r, c] = value
            else:
                acc[r, c] += value

        put(acc_g, slice(None), dot(wg[slot], x))
        put(acc_u, slice(None), dot(wu[slot], x))
        put(acc_b, slice(None), dot(wd[slot], g))
        put(acc_p, slice(0, rank), dot(pin_ref[:, x_cols], x))
        put(acc_p, slice(rank, 2 * rank), dot(pout_ref[:, g_cols], g))

    for copy in weight_copies(0, 0):
        copy.wait()

    @pl.loop(0, CHUNKS)
    def _(j):
        multiply(0, 0, j, True)

    for copy in weight_copies(2, 0):
        copy.start()

    def finish(j):
        c = chunk(j)
        units = acc_g.shape[0]
        sub = min(32, units)

        @pl.loop(0, units // sub)
        def _(i):
            r = pl.ds(pl.multiple_of(i * sub, sub), sub)
            gate, up, back = acc_g[r, c], acc_u[r, c], acc_b[r, c]
            sigma = jax.nn.sigmoid(gate)
            active = gate * sigma
            hid_s[r, :] = (active * up).astype(jnp.bfloat16)
            gg_hi[r, :], gg_lo[r, :] = split_high(back * up * sigma * (1.0 + gate * (1.0 - sigma)))
            ug_hi[r, :], ug_lo[r, :] = split_high(back * active)

        pff = pff_ref[...]
        rank = pff.shape[0]
        both = jnp.concatenate(
            [dot(pff, gg_hi[...]) + dot(pff, gg_lo[...]), dot(pff, ug_hi[...]) + dot(pff, ug_lo[...])],
            axis=0,
        )
        hidden = dot(pff, hid_s[...])
        table = table_ref[:, c]

        def outer(first, grads, inputs):
            width = grads.shape[0]
            g_hi, g_lo = (v.astype(jnp.float32) for v in split_high(grads))
            i_hi, i_lo = split_high(jnp.concatenate([inputs, inputs], axis=0))

            def masked(v):
                return jnp.concatenate(
                    [(v * table[k:k + 1, :]).astype(jnp.bfloat16) for k in range(segs)], axis=0)

            wide = dot_lanes(masked(g_hi), jnp.concatenate([i_hi, i_lo], axis=0))
            low = dot_lanes(masked(g_lo), i_hi)
            sums[first:first + segs * width, :] += (
                wide[:, :2 * rank] + (wide[:, 2 * rank:] + low))

        outer(0, both, acc_p[:rank, c])
        outer(2 * rank * segs, acc_p[rank:, c], hidden)

    @pl.loop(1, chips)
    def _(s):
        slot = lax.rem(s, 2)
        for copy in weight_copies(s, slot):
            copy.wait()

        @pl.loop(0, CHUNKS)
        def _(j):
            for copy in ring_copies(s - 1, j):
                copy.wait_recv()

            @pl.when(s < last)
            def _():
                for copy in ring_copies(s, j):
                    copy.start()

            for copy in sib_copies(s, j):
                copy.start()
            for copy in sib_copies(s, j):
                copy.wait_recv()
            multiply(s, slot, j, False)

            @pl.when(s == last)
            def _():
                finish(j)

        @pl.when(s + 2 < chips)
        def _():
            for copy in weight_copies(s + 2, slot):
                copy.start()

    rank = pff_ref.shape[0]
    lane = lax.broadcasted_iota(jnp.int32, (1, 2 * rank), 1)
    span = segs * rank
    packed[:span, :] = jnp.where(lane < rank, sums[:span, :], sums[span:2 * span, :])
    packed[span:, :] = jnp.where(
        lane < rank, sums[2 * span:2 * span + span // 2, :], sums[2 * span + span // 2:, :])

    mine = pl.ds(pl.multiple_of(core * part, part), part)
    others = pl.ds(pl.multiple_of((1 - core) * part, part), part)
    swap = remote(packed.at[others, :], sib_half, sib_sem.at[0], sib_sem.at[1], sib)
    swap.start()

    @pl.loop(0, last)
    def _(s):
        @pl.loop(0, CHUNKS)
        def _(j):
            for copy in ring_copies(s, j):
                copy.wait_send()
            for copy in sib_copies(s + 1, j):
                copy.wait_send()

    for j in range(CHUNKS):
        for k in range(2):
            for copy in pair_copies(j, k):
                copy.wait_send()

    swap.wait_recv()
    half[...] = packed[mine, :] + sib_half[...]

    def piece_rows(c):
        return pl.ds(pl.multiple_of(c * piece, piece), piece)

    def scatter(d):
        to = lax.rem(chip + d, chips)
        return remote(
            half.at[piece_rows(to), :], pieces.at[d], rs_send.at[d], rs_recv.at[d], 2 * to + core)

    for d in range(1, chips):
        scatter(d).start()
    value = half[piece_rows(chip), :]
    for d in range(1, chips):
        scatter(d).wait_recv()
        value = value + pieces[d]

    def result_rows(c, which):
        return pl.ds(pl.multiple_of(which * part + c * piece, piece), piece)

    result[result_rows(chip, core), :] = value

    def spread(d):
        r = result_rows(chip, core)
        to = 2 * lax.rem(chip + d, chips) + core
        return remote(result.at[r, :], result.at[r, :], ag_send.at[d], ag_recv.at[d], to)

    def spread_in(d):
        r = result_rows(lax.rem(chip - d + chips, chips), core)
        to = 2 * lax.rem(chip + d, chips) + core
        return remote(result.at[r, :], result.at[r, :], ag_send.at[d], ag_recv.at[d], to)

    def forward(d, which):
        r = result_rows(lax.rem(chip - d + chips, chips), which)
        return remote(result.at[r, :], result.at[r, :], fw_send.at[d], fw_recv.at[d], sib)

    for d in range(1, chips):
        spread(d).start()
    forward(0, core).start()
    for d in range(1, chips):
        spread_in(d).wait_recv()
        forward(d, core).start()
    for d in range(chips):
        forward(d, 1 - core).wait_recv()
    out_ref[...] = result[...]
    swap.wait_send()
    for d in range(1, chips):
        scatter(d).wait_send()
        spread(d).wait_send()
    for d in range(chips):
        forward(d, core).wait_send()


def fused_sums(chips, hidden_in, out_grad, w_gate, w_up, w_down, pin, pout, pff, table):
    width, total = hidden_in.shape
    units = w_gate.shape[0]
    segs = table.shape[0]
    rank = pin.shape[0]
    block = 2 * width
    rows = total // CHUNKS
    out_rows = rank * (segs + segs // 2)
    bf16, f32 = jnp.bfloat16, jnp.float32
    vmem = pl.BlockSpec(memory_space=pltpu.VMEM)
    hbm = pl.BlockSpec(memory_space=pl.ANY)
    dma = pltpu.SemaphoreType.DMA
    return pl.pallas_call(
        functools.partial(fused_kernel, chips, segs),
        out_shape=jax.ShapeDtypeStruct((out_rows, 2 * rank), f32),
        in_specs=[vmem, vmem, hbm, hbm, hbm, vmem, vmem, vmem, vmem],
        out_specs=vmem,
        scratch_shapes=[pltpu.VMEM((chips, block, total), bf16)] * 2
        + [pltpu.VMEM((units, total), f32)] * 3
        + [pltpu.VMEM((2 * rank, total), f32)]
        + [pltpu.VMEM((2, units, block), bf16)] * 3
        + [pltpu.VMEM((units, rows), bf16)] * 5
        + [
            pltpu.VMEM((2 * out_rows, 2 * rank), f32),
            pltpu.VMEM((out_rows, 2 * rank), f32),
            pltpu.VMEM((out_rows // 2, 2 * rank), f32),
            pltpu.VMEM((out_rows // 2, 2 * rank), f32),
            pltpu.VMEM((chips, out_rows // 2 // chips, 2 * rank), f32),
            pltpu.VMEM((out_rows, 2 * rank), f32),
        ]
        + [dma((2, CHUNKS))] * 4
        + [dma((chips, CHUNKS))] * 8
        + [dma((2, 3)), dma((2,))]
        + [dma((chips,))] * 6,
        compiler_params=pltpu.CompilerParams(
            collective_id=0, has_side_effects=True, vmem_limit_bytes=60 * 1024 * 1024
        ),
    )(hidden_in, out_grad, w_gate, w_up, w_down, pin, pout, pff, table)


def fused_body(hidden_in, out_grad, w_gate, w_up, w_down, proj_in, proj_ff, proj_out, lengths):
    chips = lax.axis_size("tensor") // 2
    rank = proj_in.shape[1]
    segs = lengths.shape[0]
    place = jnp.arange(segs, dtype=jnp.int32)
    ends = jnp.sum(jnp.where(place[None, :] <= place[:, None], lengths[None, :], 0), axis=1)
    starts = ends - lengths
    token = jnp.arange(hidden_in.shape[0], dtype=jnp.int32)[None, :]
    table = ((token >= starts[:, None]) & (token < ends[:, None])).astype(jnp.float32)
    sums = fused_sums(
        chips, hidden_in.T, out_grad.T, w_gate.T, w_up.T, w_down,
        proj_in.T, proj_out.T, proj_ff.T, table)
    span = segs * rank
    first = sums[:span].reshape(segs // 2, 2 * rank, 2, rank)
    second = sums[span:].reshape(segs // 2, rank, 2, rank)
    first = first.transpose(2, 0, 1, 3).reshape(segs, 2 * rank * rank)
    second = second.transpose(2, 0, 1, 3).reshape(segs, rank * rank)
    return jnp.concatenate([first, second], axis=1)


def outer_sums(table, grads, inputs):
    rows = table.shape[0]
    segs = table.shape[1]
    width = grads.shape[1]
    weighted = (table[:, :, None] * grads[:, None, :]).reshape(rows, segs * width)
    summed = jnp.dot(
        weighted.T, inputs, precision=lax.Precision.HIGHEST, preferred_element_type=jnp.float32
    )
    return summed.reshape(segs, width * inputs.shape[1])


def segment_table(lengths, start, rows):
    ends = jnp.cumsum(lengths)
    position = start + jnp.arange(rows, dtype=jnp.int32)
    segment = jnp.sum((position[:, None] >= ends[None, :]).astype(jnp.int32), axis=1)
    return (segment[:, None] == jnp.arange(lengths.shape[0], dtype=jnp.int32)[None, :]).astype(
        jnp.float32
    )


def example_sums(table, projected, in_proj, grad_proj, rank):
    hid_proj = projected[:, :rank]
    gate_proj = projected[:, rank : 2 * rank]
    up_proj = projected[:, 2 * rank : 3 * rank]
    return jnp.concatenate(
        [
            outer_sums(table, gate_proj, in_proj),
            outer_sums(table, up_proj, in_proj),
            outer_sums(table, grad_proj, hid_proj),
        ],
        axis=1,
    )


def body(hidden_in, out_grad, w_gate, w_up, w_down, proj_in, proj_ff, proj_out, lengths):
    total_rows = hidden_in.shape[0]
    units = w_gate.shape[1]
    rank = proj_in.shape[1]
    tok_share = total_rows // lax.axis_size("tensor")
    piece = lax.all_gather(hidden_in, "tensor", axis=1, tiled=True)
    pair = jnp.concatenate(
        [
            jnp.dot(piece, w_gate, preferred_element_type=jnp.float32),
            jnp.dot(piece, w_up, preferred_element_type=jnp.float32),
        ],
        axis=1,
    )
    in_proj = jnp.dot(piece, proj_in, preferred_element_type=jnp.float32)
    piece = lax.all_gather(out_grad, "tensor", axis=1, tiled=True)
    back = lax.dot_general(
        piece, w_down, (((1,), (1,)), ((), ())), preferred_element_type=jnp.float32
    )
    grad_proj = jnp.dot(piece, proj_out, preferred_element_type=jnp.float32)
    gate_pre = pair[:, :units]
    up_pre = pair[:, units:]
    sigma = jax.nn.sigmoid(gate_pre)
    active = gate_pre * sigma
    hidden = (active * up_pre).astype(jnp.bfloat16)
    gate_grad = back * up_pre * sigma * (1.0 + gate_pre * (1.0 - sigma))
    up_grad = back * active
    ff_float = proj_ff.astype(jnp.float32)
    shares = lax.psum_scatter(
        jnp.concatenate(
            [
                jnp.dot(hidden, proj_ff, preferred_element_type=jnp.float32),
                jnp.dot(
                    gate_grad,
                    ff_float,
                    precision=lax.Precision.HIGHEST,
                    preferred_element_type=jnp.float32,
                ),
                jnp.dot(
                    up_grad,
                    ff_float,
                    precision=lax.Precision.HIGHEST,
                    preferred_element_type=jnp.float32,
                ),
            ],
            axis=1,
        ),
        "tensor",
        scatter_dimension=0,
        tiled=True,
    )
    first_row = lax.axis_index("tensor") * tok_share
    table = segment_table(lengths, first_row, tok_share)
    in_part = lax.dynamic_slice_in_dim(in_proj, first_row, tok_share, 0)
    grad_part = lax.dynamic_slice_in_dim(grad_proj, first_row, tok_share, 0)
    partial_sums = example_sums(table, shares, in_part, grad_part, rank)
    result = lax.psum(partial_sums, "tensor")
    return result


def solution(mesh):
    placed = (
        P("parts", "tensor"),
        P("parts", "tensor"),
        P(None, "tensor"),
        P(None, "tensor"),
        P("tensor", None),
        P(),
        P("tensor", None),
        P(),
        P("parts"),
    )

    def either(*args):
        devices = lax.axis_size("tensor")
        fits = (
            devices == 16
            and args[0].shape[1] % 64 == 0
            and args[0].shape[0] % (256 * CHUNKS) == 0
            and args[2].shape[1] % 32 == 0
            and args[5].shape[1] == 64
            and args[8].shape[0] % 2 == 0
        )
        return (fused_body if fits else body)(*args)

    return jax.shard_map(
        either, mesh=mesh, in_specs=placed, out_specs=P("parts", None), check_vma=False
    )
```
